32 devices in a mesh: mp: 2 (over core), heads: 8 (over z, y), tok: 2 (over x).
Axes of the slice: x: 2, y: 2, z: 4, core: 2. Of those that a mesh axis runs over, the one named last changes fastest.
Arguments:
- context: bfloat16 [2, 512, 8192], P('mp', None, 'heads'), may hold values from -6 to 6
- out_weight: bfloat16 [2, 8192, 8192], P('mp', 'heads', 'tok'), may hold values from -0.0625 to 0.0625
- skip_states: bfloat16 [2, 512, 8192], P(None, None, 'tok'), may hold values from -6 to 6
- gram_old: float32 [8192, 8192], P('tok', ('mp', 'heads')), may hold values from -1 to 3
- cross_old: float32 [8192, 8192], P('tok', ('mp', 'heads')), may hold values from -30 to 30
- map_old: float32 [8192, 8192], P('tok', ('mp', 'heads')), may hold values from -0.3 to 0.3
Outputs:
- gram_new: float32 [8192, 8192], P('tok', ('mp', 'heads'))
- cross_new: float32 [8192, 8192], P('tok', ('mp', 'heads'))
- map_new: float32 [8192, 8192], P('tok', ('mp', 'heads'))
- residual_new: float32 [8192, 8192], P('tok', ('mp', 'heads'))
The draws below stay inside these ranges and needn't reach their ends.
All inputs are finite; a program needn't handle non-finite values.
Results may differ from the reference program's by a relative error of at most 0.03.
Values may be sent and summed in bfloat16 or wider, within the bound.
A program may use at most 256 MiB of HBM per device.

```python
import math
import jax
import jax.numpy as jnp
from jax import lax

D = 8192
NH = 64
HD = 128
TOKENS = 512
N_HEADS = 8


def draw_gram_old(key, part):
    first_key, second_key = jax.random.split(jax.random.fold_in(key, 11))
    highest = 2.0
    uniform_base = jax.random.uniform(first_key, (D, D), jnp.float32, -1.0, 1.0)
    off_part = (uniform_base + uniform_base.T) * (0.35 / math.sqrt(D))
    spread = jax.random.uniform(second_key, (D,), jnp.float32, 0.0, 1.0)
    diagonal = jnp.exp(spread * math.log(highest))
    row_ids = lax_iota_rows()
    on_diagonal = row_ids[:, None] == row_ids[None, :]
    return jnp.where(on_diagonal, diagonal[:, None] * jnp.ones((1, D), jnp.float32), off_part)


def lax_iota_rows():
    return jnp.arange(D, dtype=jnp.int32)


def draw_cross_old(key, part):
    keys = jax.random.split(jax.random.fold_in(key, 23), 3)
    row_scale = jnp.exp(jax.random.uniform(keys[0], (D,), jnp.float32, 0.0, 1.0) * math.log(10.0))
    col_scale = jnp.exp(jax.random.uniform(keys[1], (D,), jnp.float32, 0.0, 1.0) * math.log(10.0))
    ramp = jnp.exp(0.5 * math.log(3.0) * jnp.arange(D, dtype=jnp.float32) / D)
    values = jnp.clip(jax.random.normal(keys[2], (D, D), jnp.float32), -4.0, 4.0)
    return 0.02 * values * (row_scale * ramp)[:, None] * (col_scale * ramp)[None, :]


def shard_levels(rng, dims, pieces, low, top_value):
    def one(dim, parts):
        draws = jax.random.uniform(jax.random.fold_in(jax.random.fold_in(rng, 6), dim), (parts,), jnp.float32, low / len(pieces), top_value / len(pieces))
        return jnp.repeat(jnp.exp(draws), dims[dim] // parts).reshape((-1,) + (1,) * (len(dims) - dim - 1))

    level = one(*pieces[0])
    for cut in pieces[1:]:
        level = level * one(*cut)
    return level


def bell_draw(rng, extent, width, limit, shards=(), kind=jnp.bfloat16):
    result = width * jax.random.normal(rng, extent, jnp.float32)
    if shards:
        result = result * shard_levels(rng, extent, shards, -0.22, 0.18)
    return jnp.clip(result, -limit, limit).astype(kind)


def setup_inputs(seed: int = 0) -> dict:
    splits = jax.random.split(jax.random.key(seed), 7)
    context = bell_draw(splits[0], (2, TOKENS, NH * HD), 1.0, 6.0, ((0, 2), (2, 8)))
    out_weight = bell_draw(splits[1], (2, NH * HD, D), (NH * HD) ** -0.5, 0.0625, ((0, 2), (1, 8), (2, 2)))
    skip_states = bell_draw(splits[2], (2, TOKENS, D), 1.0, 6.0, ((2, 2),))
    gram_old = draw_gram_old(jax.random.fold_in(splits[6], 71), 0)
    cross_old = draw_cross_old(jax.random.fold_in(splits[6], 71), 0)
    map_old = bell_draw(splits[5], (D, D), 0.05, 0.3, ((0, 2), (1, 16)), jnp.float32)
    return dict(context=context, out_weight=out_weight, skip_states=skip_states, gram_old=gram_old, cross_old=cross_old, map_old=map_old)


decay_keep = 0.75
ridge_weight = 0.1


def model_states(context_one, weight_one, skip_one):
    group_width = context_one.shape[1] // N_HEADS
    running = jnp.zeros((context_one.shape[0], weight_one.shape[1]), jnp.float32)
    for group_index in range(N_HEADS):
        lower = group_index * group_width
        portion = jnp.dot(context_one[:, lower:lower + group_width], weight_one[lower:lower + group_width, :], preferred_element_type=jnp.float32)
        rounded = lax.optimization_barrier(portion.astype(jnp.bfloat16))
        running = running + rounded.astype(jnp.float32)
    return (running + skip_one.astype(jnp.float32)).astype(jnp.bfloat16)


def reference(context, out_weight, skip_states, gram_old, cross_old, map_old):
    source = model_states(context[0], out_weight[0], skip_states[0])
    target = model_states(context[1], out_weight[1], skip_states[1])
    new_weight = (1.0 - decay_keep) / TOKENS
    gram_new = decay_keep * gram_old + new_weight * jnp.dot(source.T, source, preferred_element_type=jnp.float32)
    cross_new = decay_keep * cross_old + new_weight * jnp.dot(source.T, target, preferred_element_type=jnp.float32)
    gram_half = gram_new.astype(jnp.bfloat16)
    map_half = map_old.astype(jnp.bfloat16)
    residual = cross_new - jnp.dot(gram_half, map_half, preferred_element_type=jnp.float32) - ridge_weight * map_old
    residual_half = residual.astype(jnp.bfloat16)
    applied = jnp.dot(gram_half, residual_half, preferred_element_type=jnp.float32) + ridge_weight * residual
    step_size = jnp.sum(residual * residual) / jnp.sum(residual * applied)
    map_new = map_old + step_size * residual
    residual_new = residual - step_size * applied
    return (gram_new, cross_new, map_new, residual_new)
```

```python
import jax
import jax.numpy as jnp
from jax import lax
from jax.sharding import PartitionSpec as P

decay_keep = 0.75
ridge_weight = 0.1
f32, bf16 = jnp.float32, jnp.bfloat16
CHUNKS = 4


def dot(a, b):
    return jnp.dot(a, b, preferred_element_type=f32)


def token_inner(left, right):
    return lax.dot_general(left, right, (((0,), (0,)), ((), ())), preferred_element_type=f32)


def shifted(block, axis, shift):
    n = lax.axis_size(axis)
    return lax.ppermute(block, axis, [(i, (i + shift) % n) for i in range(n)])


def total_over(value, axis):
    n = lax.axis_size(axis)
    if n & (n - 1):
        return lax.psum(value, axis)
    bit = 1
    while bit < n:
        value = value + lax.ppermute(value, axis, [(i, i ^ bit) for i in range(n)])
        bit *= 2
    return value


def sum_tok(value):
    n = lax.axis_size("tok")
    half = value.astype(bf16)
    for shift in range(1, n):
        value = value + shifted(half, "tok", shift).astype(f32)
    return value.astype(bf16)


def scatter_sum(part, axis):
    n = lax.axis_size(axis)
    me = lax.axis_index(axis)
    share = part.shape[1] // n
    blocks = [part[:, i * share:(i + 1) * share] for i in range(n)]
    bit = 1
    while bit < n:
        mine = (me // bit) % 2 == 1
        keep = [jnp.where(mine, high, low) for low, high in zip(blocks[0::2], blocks[1::2])]
        send = [jnp.where(mine, low, high) for low, high in zip(blocks[0::2], blocks[1::2])]
        send = jnp.concatenate([block.astype(bf16) for block in send], 1)
        got = lax.ppermute(send, axis, [(i, i ^ bit) for i in range(n)]).astype(f32)
        blocks = [block.astype(f32) + got[:, i * share:(i + 1) * share] for i, block in enumerate(keep)]
        bit *= 2
    return blocks[0]


def gather_columns(block, axis):
    n = lax.axis_size(axis)
    me = lax.axis_index(axis)
    bit = n // 2
    blocks = [block]
    while bit:
        mine = (me // bit) % 2 == 1
        own = jnp.concatenate(blocks, 1)
        got = lax.ppermute(own, axis, [(i, i ^ bit) for i in range(n)])
        share = block.shape[1]
        got = [got[:, i * share:(i + 1) * share] for i in range(len(blocks))]
        low = [jnp.where(mine, g, o) for g, o in zip(got, blocks)]
        high = [jnp.where(mine, o, g) for g, o in zip(got, blocks)]
        blocks = [x for pair in zip(low, high) for x in pair]
        bit //= 2
    return jnp.concatenate(blocks, 1)


def make_states(context, out_weight, skip_states, width):
    n_tok, n_heads, n_mp = (lax.axis_size(a) for a in ("tok", "heads", "mp"))
    t, h, k = (lax.axis_index(a) for a in ("tok", "heads", "mp"))
    tokens, features = skip_states.shape[1:]
    share = features // n_heads
    part = dot(context[0], out_weight[0]).astype(bf16)
    mine = scatter_sum(part, "heads")
    skip = lax.dynamic_slice(skip_states, (k, 0, h * share), (1, tokens, share))[0]
    mine = (mine + skip.astype(f32)).astype(bf16)
    other = lax.ppermute(mine, "mp", [(0, 1), (1, 0)])
    pair = jnp.stack([jnp.where(k == 0, mine, other), jnp.where(k == 0, other, mine)])
    if share == width and n_tok == n_mp == 2:
        away = lax.ppermute(pair, ("mp", "tok"), [(0, 1), (3, 2)])
        columns = jnp.where(k == t, pair, away)
        half = lax.dynamic_slice_in_dim(pair[0], k * (tokens // 2), tokens // 2, 0)
        rows = gather_columns(half, "heads")
        rows_other = lax.ppermute(rows, "mp", [(0, 1), (1, 0)])
        first = jnp.where(k == 0, rows, rows_other)
        second = jnp.where(k == 0, rows_other, rows)
        source = jnp.concatenate([first, second], 0)
        return source, columns[0], columns[1]
    both = lax.all_gather(pair, "heads", axis=2, tiled=True)
    whole = lax.all_gather(both, "tok", axis=2, tiled=True)
    columns = lax.dynamic_slice_in_dim(whole, (k * n_heads + h) * width, width, 2)
    return both[0], columns[0], columns[1]


def per_device(context, out_weight, skip_states, gram_old, cross_old, map_old):
    n_tok = lax.axis_size("tok")
    t = lax.axis_index("tok")
    tokens = context.shape[1]
    height, width = gram_old.shape
    new_weight = (1.0 - decay_keep) / tokens
    step = height // CHUNKS
    cuts = [slice(c * step, (c + 1) * step) for c in range(CHUNKS)]

    def by_owner(blocks):
        if n_tok == 2:
            own, other = blocks
            return [jnp.where(t == 0, own, other), jnp.where(t == 0, other, own)]
        stacked = jnp.stack(blocks)
        return [
            lax.dynamic_index_in_dim(stacked, lax.rem(t - o + n_tok, n_tok), 0, keepdims=False)
            for o in range(n_tok)
        ]

    def all_shifts(block):
        return [block] + [shifted(block, "tok", s) for s in range(1, n_tok)]

    panels = [
        lax.all_gather(gram_old[cut].astype(bf16), ("mp", "heads"), axis=1, tiled=True) for cut in cuts
    ]
    maps = by_owner(all_shifts(map_old.astype(bf16)))
    source, source_cols, target_cols = make_states(context, out_weight, skip_states, width)
    gram_new = decay_keep * gram_old + new_weight * token_inner(source, source_cols)
    cross_new = decay_keep * cross_old + new_weight * token_inner(source, target_cols)
    inner_map = sum_tok(dot(source, map_old.astype(bf16)))

    residuals, halves, inner_parts = [], [], []
    strips = []
    applied = [None] * CHUNKS
    for r, cut in enumerate(cuts):
        panel = panels[r]
        product = sum(dot(panel[:, o * height:(o + 1) * height], maps[o]) for o in range(n_tok))
        low_rank = token_inner(source[:, cut], inner_map)
        residual = (
            cross_new[cut] - decay_keep * product - new_weight * low_rank - ridge_weight * map_old[cut]
        )
        residuals.append(residual)
        half = residual.astype(bf16)
        inner_parts.append(dot(source[:, cut], half))
        strips.append(by_owner(all_shifts(half)))
        for i in range(r):
            for o in range(n_tok):
                begin = o * height + r * step
                applied[i] = applied[i] + dot(panels[i][:, begin:begin + step], strips[r][o])
        for o in range(n_tok):
            known = strips[0][o] if r == 0 else jnp.concatenate([s[o] for s in strips], 0)
            value = dot(panel[:, o * height:o * height + (r + 1) * step], known)
            applied[r] = value if applied[r] is None else applied[r] + value
    inner_residual = sum_tok(sum(inner_parts))
    squares, mixed = 0.0, 0.0
    values = []
    for cut, residual, product in zip(cuts, residuals, applied):
        low_rank = token_inner(source[:, cut], inner_residual)
        value = decay_keep * product + new_weight * low_rank + ridge_weight * residual
        values.append(value)
        squares = squares + jnp.sum(residual * residual)
        mixed = mixed + jnp.sum(residual * value)
    totals = jnp.stack([squares, mixed])
    for axis in ("mp", "tok", "heads"):
        totals = total_over(totals, axis)
    step_size = totals[0] / totals[1]
    residual = jnp.concatenate(residuals, 0)
    return (
        gram_new,
        cross_new,
        map_old + step_size * residual,
        residual - step_size * jnp.concatenate(values, 0),
    )


def solution(mesh):
    block = P("tok", ("mp", "heads"))
    placed = (P("mp", None, "heads"), P("mp", "heads", "tok"), P(None, None, "tok"), block, block, block)
    return jax.shard_map(
        per_device, mesh=mesh, in_specs=placed, out_specs=(block,) * 4, check_vma=False
    )
```

```python
import jax
import jax.numpy as jnp
from jax import lax
from jax.experimental import pallas as pl
from jax.experimental.pallas import tpu as pltpu
from jax.sharding import PartitionSpec as P

decay_keep = 0.75
ridge_weight = 0.1
f32, bf16 = jnp.float32, jnp.bfloat16
CHUNKS = 4


def dot(a, b):
    return jnp.dot(a, b, preferred_element_type=f32)


def token_inner(left, right):
    return lax.dot_general(left, right, (((0,), (0,)), ((), ())), preferred_element_type=f32)


def shifted(block, axis, shift):
    n = lax.axis_size(axis)
    return lax.ppermute(block, axis, [(i, (i + shift) % n) for i in range(n)])


def total_over(value, axis):
    n = lax.axis_size(axis)
    if n & (n - 1):
        return lax.psum(value, axis)
    bit = 1
    while bit < n:
        value = value + lax.ppermute(value, axis, [(i, i ^ bit) for i in range(n)])
        bit *= 2
    return value


def sum_tok(value):
    n = lax.axis_size("tok")
    half = value.astype(bf16)
    for shift in range(1, n):
        value = value + shifted(half, "tok", shift).astype(f32)
    return value.astype(bf16)


def scatter_sum(part, axis):
    n = lax.axis_size(axis)
    me = lax.axis_index(axis)
    share = part.shape[1] // n
    blocks = [part[:, i * share:(i + 1) * share] for i in range(n)]
    bit = 1
    while bit < n:
        mine = (me // bit) % 2 == 1
        keep = [jnp.where(mine, high, low) for low, high in zip(blocks[0::2], blocks[1::2])]
        send = [jnp.where(mine, low, high) for low, high in zip(blocks[0::2], blocks[1::2])]
        send = jnp.concatenate([block.astype(bf16) for block in send], 1)
        got = lax.ppermute(send, axis, [(i, i ^ bit) for i in range(n)]).astype(f32)
        blocks = [block.astype(f32) + got[:, i * share:(i + 1) * share] for i, block in enumerate(keep)]
        bit *= 2
    return blocks[0]


def gather_columns(block, axis):
    n = lax.axis_size(axis)
    me = lax.axis_index(axis)
    bit = n // 2
    blocks = [block]
    while bit:
        mine = (me // bit) % 2 == 1
        own = jnp.concatenate(blocks, 1)
        got = lax.ppermute(own, axis, [(i, i ^ bit) for i in range(n)])
        share = block.shape[1]
        got = [got[:, i * share:(i + 1) * share] for i in range(len(blocks))]
        low = [jnp.where(mine, g, o) for g, o in zip(got, blocks)]
        high = [jnp.where(mine, o, g) for g, o in zip(got, blocks)]
        blocks = [x for pair in zip(low, high) for x in pair]
        bit //= 2
    return jnp.concatenate(blocks, 1)


def make_states(context, out_weight, skip_states, width):
    n_tok, n_heads, n_mp = (lax.axis_size(a) for a in ("tok", "heads", "mp"))
    t, h, k = (lax.axis_index(a) for a in ("tok", "heads", "mp"))
    tokens, features = skip_states.shape[1:]
    share = features // n_heads
    part = dot(context[0], out_weight[0]).astype(bf16)
    mine = scatter_sum(part, "heads")
    skip = lax.dynamic_slice(skip_states, (k, 0, h * share), (1, tokens, share))[0]
    mine = (mine + skip.astype(f32)).astype(bf16)
    other = lax.ppermute(mine, "mp", [(0, 1), (1, 0)])
    pair = jnp.stack([jnp.where(k == 0, mine, other), jnp.where(k == 0, other, mine)])
    if share == width and n_tok == n_mp == 2:
        away = lax.ppermute(pair, ("mp", "tok"), [(0, 1), (3, 2)])
        columns = jnp.where(k == t, pair, away)
        half = lax.dynamic_slice_in_dim(pair[0], k * (tokens // 2), tokens // 2, 0)
        rows = gather_columns(half, "heads")
        rows_other = lax.ppermute(rows, "mp", [(0, 1), (1, 0)])
        first = jnp.where(k == 0, rows, rows_other)
        second = jnp.where(k == 0, rows_other, rows)
        source = jnp.concatenate([first, second], 0)
        return source, columns[0], columns[1]
    both = lax.all_gather(pair, "heads", axis=2, tiled=True)
    whole = lax.all_gather(both, "tok", axis=2, tiled=True)
    columns = lax.dynamic_slice_in_dim(whole, (k * n_heads + h) * width, width, 2)
    return both[0], columns[0], columns[1]


def per_device(context, out_weight, skip_states, gram_old, cross_old, map_old):
    n_tok = lax.axis_size("tok")
    t = lax.axis_index("tok")
    tokens = context.shape[1]
    height, width = gram_old.shape
    new_weight = (1.0 - decay_keep) / tokens
    step = height // CHUNKS
    cuts = [slice(c * step, (c + 1) * step) for c in range(CHUNKS)]

    map_half = map_old.astype(bf16)
    gram_old_half = gram_old.astype(bf16)
    gram_old_half, context = lax.optimization_barrier((gram_old_half, context))
    panel = lax.all_gather(gram_old_half, ("mp", "heads"), axis=1, tiled=True)
    maps = [map_half] + [shifted(map_half, "tok", s) for s in range(1, n_tok)]
    source, source_cols, target_cols = make_states(context, out_weight, skip_states, width)

    gram_new = decay_keep * gram_old + new_weight * token_inner(source, source_cols)
    cross_new = decay_keep * cross_old + new_weight * token_inner(source, target_cols)

    def panel_part(cut, s):
        owner = lax.rem(t - s + n_tok, n_tok)
        return lax.dynamic_slice(panel, (cut.start, owner * height), (step, height))

    inner_map = sum_tok(dot(source, map_half))
    residuals, halves = [], []
    for cut in cuts:
        product = sum(dot(panel_part(cut, s), maps[s]) for s in range(n_tok))
        low_rank = token_inner(source[:, cut], inner_map)
        residual = (
            cross_new[cut] - decay_keep * product - new_weight * low_rank - ridge_weight * map_old[cut]
        )
        residuals.append(residual)
        halves.append(residual.astype(bf16))
    away = [[shifted(half, "tok", s) for half in halves] for s in range(1, n_tok)]
    inner_residual = sum_tok(sum(dot(source[:, cut], half) for cut, half in zip(cuts, halves)))
    blocks = [jnp.concatenate(halves, 0)] + [jnp.concatenate(a, 0) for a in away]
    applied, squares, mixed = [], 0.0, 0.0
    for cut, residual in zip(cuts, residuals):
        product = sum(dot(panel_part(cut, s), blocks[s]) for s in range(n_tok))
        low_rank = token_inner(source[:, cut], inner_residual)
        value = decay_keep * product + new_weight * low_rank + ridge_weight * residual
        applied.append(value)
        squares = squares + jnp.sum(residual * residual)
        mixed = mixed + jnp.sum(residual * value)
    totals = jnp.stack([squares, mixed])
    for axis in ("mp", "tok", "heads"):
        totals = total_over(totals, axis)
    step_size = totals[0] / totals[1]
    residual = jnp.concatenate(residuals, 0)
    return (
        gram_new,
        cross_new,
        map_old + step_size * residual,
        residual - step_size * jnp.concatenate(applied, 0),
    )


UNITS = 16
LATER = 48
MESH = pl.DeviceIdType.MESH


def gather_kernel(
    g_ref, m_hbm, base_hbm, panel, res_hbm, app_hbm,
    maps, rf, acc, prod, buf, col, base, own_sem, in_sem, col_sem, out_sem, zs, zr, ys, yr, bs, br, cs, cr, xs, xr,
):
    k, h, t = lax.axis_index("mp"), lax.axis_index("heads"), lax.axis_index("tok")
    z, y = h // 2, h % 2
    height, width = g_ref.shape
    unit = height // UNITS
    early = unit - LATER
    chunks = rf.shape[0] // 2
    step = height // chunks
    steps = ((1, 0), (-1, 1))

    def block(zz, yy):
        return k * 8 + zz * 2 + yy

    def inside(zz):
        return (zz >= 0) & (zz <= 3)

    def piece(zz, yy, u, lo, n):
        return panel.at[block(zz, yy), pl.ds(pl.multiple_of(u * unit, unit) + lo, n)]

    def remote(ref, send, recv, dev):
        return pltpu.make_async_remote_copy(
            src_ref=ref, dst_ref=ref, send_sem=send, recv_sem=recv, device_id=dev, device_id_type=MESH
        )

    def at_z(dz):
        return (k, jnp.clip(z + dz, 0, 3) * 2 + y, t)

    at_y = (k, z * 2 + 1 - y, t)
    at_core = (1 - k, h, t)
    at_x = (k, h, 1 - t)

    def z_copy(s, dz, d, zz, u):
        return remote(piece(jnp.clip(zz, 0, 3), y, u, 0, unit), zs.at[d, s, u], zr.at[d, s, u], at_z(dz))

    def b_copy(s, dz, d, zz, u):
        return remote(
            piece(jnp.clip(zz, 0, 3), 1 - y, u, early, LATER), bs.at[d, s, u], br.at[d, s, u], at_z(dz)
        )

    def y_copy(zz, yy, u, n):
        zz = jnp.clip(zz, 0, 3)
        return remote(piece(zz, yy, u, 0, n), ys.at[zz, u], yr.at[zz, u], at_y)

    def core_copy(kk, u):
        ref = panel.at[pl.ds(kk * 8, 8), pl.ds(pl.multiple_of(u * unit, unit), unit)]
        return remote(ref, cs.at[u], cr.at[u], at_core)

    def x_copy(tt, c):
        return remote(rf.at[tt * chunks + c], xs.at[c], xr.at[c], at_x)

    own = pltpu.make_async_copy(g_ref, panel.at[block(z, y)], own_sem)
    own.start()
    load_maps = pltpu.make_async_copy(m_hbm, maps, in_sem)
    load_maps.start()
    barrier = pltpu.get_barrier_semaphore()
    for dev in (at_y, at_core, at_x):
        pl.semaphore_signal(barrier, inc=1, device_id=dev, device_id_type=MESH)
    for dz, d in steps:
        @pl.when(inside(z + dz))
        def _():
            pl.semaphore_signal(barrier, inc=1, device_id=at_z(dz), device_id_type=MESH)
    pl.semaphore_wait(barrier, 3 + jnp.where(z > 0, 1, 0) + jnp.where(z < 3, 1, 0))
    own.wait()
    load_maps.wait()

    def valid(u):
        return (u >= 0) & (u < UNITS)

    def product_one(c):
        for half in range(2):
            core_copy(1 - k, 2 * c + half).wait_recv()
        rows = pl.ds(pl.multiple_of(c * step, step), step)
        load = pltpu.make_async_copy(panel.at[:, rows], buf, in_sem)
        load.start()
        load_base = pltpu.make_async_copy(base_hbm.at[rows], base, own_sem)
        load_base.start()
        load.wait()
        prod[...] = jnp.zeros_like(prod)

        @pl.loop(0, 8)
        def _(q):
            prod[...] += jnp.dot(buf[2 * q], maps[2 * q], preferred_element_type=f32) + jnp.dot(
                buf[2 * q + 1], maps[2 * q + 1], preferred_element_type=f32
            )

        load_base.wait()
        base[...] = base[...] - decay_keep * prod[...]
        rf[t * chunks + c] = base[...].astype(bf16)
        x_copy(t, c).start()
        save = pltpu.make_async_copy(base, res_hbm.at[rows], out_sem)
        save.start()
        prod[...] = jnp.zeros_like(prod)

        @pl.loop(0, c)
        def _(i):
            prod[...] += jnp.dot(buf[i], rf[i], preferred_element_type=f32) + jnp.dot(
                buf[chunks + i], rf[chunks + i], preferred_element_type=f32
            )

        acc[c] = prod[...]
        save.wait()

    def column(c, i, slot, o):
        return pltpu.make_async_copy(
            panel.at[o * chunks + c, pl.ds(pl.multiple_of(i * step, step), step)],
            col.at[slot, o],
            col_sem.at[slot, o],
        )

    def product_two(c):
        for o in range(2):
            column(c, 0, 0, o).start()
        x_copy(1 - t, c).wait_recv()

        @pl.loop(0, c + 1)
        def _(i):
            slot = i % 2

            @pl.when(i < c)
            def _():
                for o in range(2):
                    column(c, i + 1, 1 - slot, o).start()

            for o in range(2):
                column(c, i, slot, o).wait()
            acc[i] += jnp.dot(col[slot, 0], rf[c], preferred_element_type=f32) + jnp.dot(
                col[slot, 1], rf[chunks + c], preferred_element_type=f32
            )

    @pl.loop(0, UNITS + 6)
    def _(tick):
        u0 = tick

        @pl.when(u0 < UNITS)
        def _():
            for dz, d in steps:
                @pl.when(inside(z + dz))
                def _():
                    z_copy(0, dz, d, z, u0).start()
            y_copy(z, y, u0, unit).start()

        for lag in range(1, 5):
            u = tick - lag

            @pl.when(valid(u))
            def _():
                if lag <= 3:
                    for dz, d in steps:
                        zz = z - lag * dz

                        @pl.when(inside(zz))
                        def _():
                            z_copy(lag - 1, dz, d, zz, u).wait_recv()
                            if lag < 3:
                                @pl.when(inside(z + dz))
                                def _():
                                    z_copy(lag, dz, d, zz, u).start()
                            y_copy(zz, y, u, early).start()
                if lag == 1:
                    y_copy(z, 1 - y, u, unit).wait_recv()
                    for dz, d in steps:
                        @pl.when(inside(z + dz))
                        def _():
                            b_copy(0, dz, d, z, u).start()
                else:
                    for dz, d in steps:
                        zz = z - (lag - 1) * dz

                        @pl.when(inside(zz))
                        def _():
                            y_copy(zz, 1 - y, u, early).wait_recv()
                            b_copy(lag - 2, dz, d, zz, u).wait_recv()
                            if lag < 4:
                                @pl.when(inside(z + dz))
                                def _():
                                    b_copy(lag - 1, dz, d, zz, u).start()
                if lag == 4:
                    core_copy(k, u).start()

        w = tick - 6

        @pl.when((w >= 0) & (w % 2 == 0))
        def _():
            product_one(w // 2)

        @pl.when((w >= 0) & (w % 2 == 1))
        def _():
            product_two(w // 2)

    save = pltpu.make_async_copy(acc, app_hbm, out_sem)
    save.start()

    @pl.loop(0, UNITS)
    def _(u):
        for s in range(3):
            for dz, d in steps:
                @pl.when(inside(z - s * dz) & inside(z + dz))
                def _():
                    z_copy(s, dz, d, z - s * dz, u).wait_send()
                    b_copy(s, dz, d, z - s * dz, u).wait_send()
        y_copy(z, y, u, unit).wait_send()
        for s in range(1, 4):
            for dz, d in steps:
                @pl.when(inside(z - s * dz))
                def _():
                    y_copy(z - s * dz, y, u, early).wait_send()
        core_copy(k, u).wait_send()

    @pl.loop(0, chunks)
    def _(c):
        x_copy(t, c).wait_send()

    save.wait()


def gather_and_multiply(gram_half, maps, base):
    height, width = gram_half.shape
    chunks = 8
    step = height // chunks
    any_space = pl.BlockSpec(memory_space=pltpu.HBM)
    dma = pltpu.SemaphoreType.DMA
    panel, residual, applied = pl.pallas_call(
        gather_kernel,
        out_shape=[
            jax.ShapeDtypeStruct((16, height, width), bf16),
            jax.ShapeDtypeStruct((height, width), f32),
            jax.ShapeDtypeStruct((chunks, step, width), f32),
        ],
        in_specs=[any_space] * 3,
        out_specs=[any_space] * 3,
        scratch_shapes=[
            pltpu.VMEM((16, step, width), bf16),
            pltpu.VMEM((16, step, width), bf16),
            pltpu.VMEM((chunks, step, width), f32),
            pltpu.VMEM((step, width), f32),
            pltpu.VMEM((16, step, width), bf16),
            pltpu.VMEM((2, 2, step, width), bf16),
            pltpu.VMEM((step, width), f32),
            dma, dma, dma((2, 2)), dma,
            dma((2, 3, UNITS)), dma((2, 3, UNITS)),
            dma((4, UNITS)), dma((4, UNITS)),
            dma((2, 3, UNITS)), dma((2, 3, UNITS)),
            dma((UNITS,)), dma((UNITS,)),
            dma((chunks,)), dma((chunks,)),
        ],
        compiler_params=pltpu.CompilerParams(
            collective_id=0, has_side_effects=True, vmem_limit_bytes=56 * 1024 * 1024
        ),
        cost_estimate=pl.CostEstimate(
            flops=4 * height * width * 16 * width, bytes_accessed=16 * height * width * 6, transcendentals=0
        ),
    )(gram_half, maps.reshape(16, step, width), base)
    return residual, applied.reshape(height, width)


def with_kernel(context, out_weight, skip_states, gram_old, cross_old, map_old):
    t = lax.axis_index("tok")
    tokens = context.shape[1]
    width = gram_old.shape[1]
    new_weight = (1.0 - decay_keep) / tokens
    map_half = map_old.astype(bf16)
    map_away = shifted(map_half, "tok", 1)
    maps = jnp.concatenate(
        [jnp.where(t == 0, map_half, map_away), jnp.where(t == 0, map_away, map_half)], 0
    )
    source, source_cols, target_cols = make_states(context, out_weight, skip_states, width)
    inner_map = sum_tok(dot(source, map_half))
    cross_new = decay_keep * cross_old + new_weight * token_inner(source, target_cols)
    base = cross_new - new_weight * token_inner(source, inner_map) - ridge_weight * map_old
    residual, product = gather_and_multiply(gram_old.astype(bf16), maps, base)
    gram_new = decay_keep * gram_old + new_weight * token_inner(source, source_cols)
    inner_residual = sum_tok(dot(source, residual.astype(bf16)))
    applied = decay_keep * product + new_weight * token_inner(source, inner_residual) + ridge_weight * residual
    totals = jnp.stack([jnp.sum(residual * residual), jnp.sum(residual * applied)])
    for axis in ("mp", "tok", "heads"):
        totals = total_over(totals, axis)
    step_size = totals[0] / totals[1]
    return gram_new, cross_new, map_old + step_size * residual, residual - step_size * applied


def solution(mesh):
    block = P("tok", ("mp", "heads"))
    placed = (P("mp", None, "heads"), P("mp", "heads", "tok"), P(None, None, "tok"), block, block, block)
    lines = dict(mesh.shape) == {"mp": 2, "heads": 8, "tok": 2}
    return jax.shard_map(
        with_kernel if lines else per_device,
        mesh=mesh, in_specs=placed, out_specs=(block,) * 4, check_vma=False,
    )
```

```python
import jax
import jax.numpy as jnp
from jax import lax
from jax.experimental import pallas as pl
from jax.experimental.pallas import tpu as pltpu
from jax.sharding import PartitionSpec as P

decay_keep = 0.75
ridge_weight = 0.1
f32, bf16 = jnp.float32, jnp.bfloat16
CHUNKS = 4


def dot(a, b):
    return jnp.dot(a, b, preferred_element_type=f32)


def token_inner(left, right):
    return lax.dot_general(left, right, (((0,), (0,)), ((), ())), preferred_element_type=f32)


def shifted(block, axis, shift):
    n = lax.axis_size(axis)
    return lax.ppermute(block, axis, [(i, (i + shift) % n) for i in range(n)])


def total_over(value, axis):
    n = lax.axis_size(axis)
    if n & (n - 1):
        return lax.psum(value, axis)
    bit = 1
    while bit < n:
        value = value + lax.ppermute(value, axis, [(i, i ^ bit) for i in range(n)])
        bit *= 2
    return value


def sum_tok(value):
    n = lax.axis_size("tok")
    half = value.astype(bf16)
    for shift in range(1, n):
        value = value + shifted(half, "tok", shift).astype(f32)
    return value.astype(bf16)


def scatter_sum(part, axis):
    n = lax.axis_size(axis)
    me = lax.axis_index(axis)
    share = part.shape[1] // n
    blocks = [part[:, i * share:(i + 1) * share] for i in range(n)]
    bit = 1
    while bit < n:
        mine = (me // bit) % 2 == 1
        keep = [jnp.where(mine, high, low) for low, high in zip(blocks[0::2], blocks[1::2])]
        send = [jnp.where(mine, low, high) for low, high in zip(blocks[0::2], blocks[1::2])]
        send = jnp.concatenate([block.astype(bf16) for block in send], 1)
        got = lax.ppermute(send, axis, [(i, i ^ bit) for i in range(n)]).astype(f32)
        blocks = [block.astype(f32) + got[:, i * share:(i + 1) * share] for i, block in enumerate(keep)]
        bit *= 2
    return blocks[0]


def gather_columns(block, axis):
    n = lax.axis_size(axis)
    me = lax.axis_index(axis)
    bit = n // 2
    blocks = [block]
    while bit:
        mine = (me // bit) % 2 == 1
        own = jnp.concatenate(blocks, 1)
        got = lax.ppermute(own, axis, [(i, i ^ bit) for i in range(n)])
        share = block.shape[1]
        got = [got[:, i * share:(i + 1) * share] for i in range(len(blocks))]
        low = [jnp.where(mine, g, o) for g, o in zip(got, blocks)]
        high = [jnp.where(mine, o, g) for g, o in zip(got, blocks)]
        blocks = [x for pair in zip(low, high) for x in pair]
        bit //= 2
    return jnp.concatenate(blocks, 1)


def make_states(context, out_weight, skip_states, width):
    n_tok, n_heads, n_mp = (lax.axis_size(a) for a in ("tok", "heads", "mp"))
    t, h, k = (lax.axis_index(a) for a in ("tok", "heads", "mp"))
    tokens, features = skip_states.shape[1:]
    share = features // n_heads
    part = dot(context[0], out_weight[0]).astype(bf16)
    mine = scatter_sum(part, "heads")
    skip = lax.dynamic_slice(skip_states, (k, 0, h * share), (1, tokens, share))[0]
    mine = (mine + skip.astype(f32)).astype(bf16)
    other = lax.ppermute(mine, "mp", [(0, 1), (1, 0)])
    pair = jnp.stack([jnp.where(k == 0, mine, other), jnp.where(k == 0, other, mine)])
    if share == width and n_tok == n_mp == 2:
        away = lax.ppermute(pair, ("mp", "tok"), [(0, 1), (3, 2)])
        columns = jnp.where(k == t, pair, away)
        half = lax.dynamic_slice_in_dim(pair[0], k * (tokens // 2), tokens // 2, 0)
        rows = gather_columns(half, "heads")
        rows_other = lax.ppermute(rows, "mp", [(0, 1), (1, 0)])
        first = jnp.where(k == 0, rows, rows_other)
        second = jnp.where(k == 0, rows_other, rows)
        source = jnp.concatenate([first, second], 0)
        return source, columns[0], columns[1]
    both = lax.all_gather(pair, "heads", axis=2, tiled=True)
    whole = lax.all_gather(both, "tok", axis=2, tiled=True)
    columns = lax.dynamic_slice_in_dim(whole, (k * n_heads + h) * width, width, 2)
    return both[0], columns[0], columns[1]


def per_device(context, out_weight, skip_states, gram_old, cross_old, map_old):
    n_tok = lax.axis_size("tok")
    t = lax.axis_index("tok")
    tokens = context.shape[1]
    height, width = gram_old.shape
    new_weight = (1.0 - decay_keep) / tokens
    step = height // CHUNKS
    cuts = [slice(c * step, (c + 1) * step) for c in range(CHUNKS)]

    map_half = map_old.astype(bf16)
    gram_old_half = gram_old.astype(bf16)
    gram_old_half, context = lax.optimization_barrier((gram_old_half, context))
    panel = lax.all_gather(gram_old_half, ("mp", "heads"), axis=1, tiled=True)
    maps = [map_half] + [shifted(map_half, "tok", s) for s in range(1, n_tok)]
    source, source_cols, target_cols = make_states(context, out_weight, skip_states, width)

    gram_new = decay_keep * gram_old + new_weight * token_inner(source, source_cols)
    cross_new = decay_keep * cross_old + new_weight * token_inner(source, target_cols)

    def panel_part(cut, s):
        owner = lax.rem(t - s + n_tok, n_tok)
        return lax.dynamic_slice(panel, (cut.start, owner * height), (step, height))

    inner_map = sum_tok(dot(source, map_half))
    residuals, halves = [], []
    for cut in cuts:
        product = sum(dot(panel_part(cut, s), maps[s]) for s in range(n_tok))
        low_rank = token_inner(source[:, cut], inner_map)
        residual = (
            cross_new[cut] - decay_keep * product - new_weight * low_rank - ridge_weight * map_old[cut]
        )
        residuals.append(residual)
        halves.append(residual.astype(bf16))
    away = [[shifted(half, "tok", s) for half in halves] for s in range(1, n_tok)]
    inner_residual = sum_tok(sum(dot(source[:, cut], half) for cut, half in zip(cuts, halves)))
    blocks = [jnp.concatenate(halves, 0)] + [jnp.concatenate(a, 0) for a in away]
    applied, squares, mixed = [], 0.0, 0.0
    for cut, residual in zip(cuts, residuals):
        product = sum(dot(panel_part(cut, s), blocks[s]) for s in range(n_tok))
        low_rank = token_inner(source[:, cut], inner_residual)
        value = decay_keep * product + new_weight * low_rank + ridge_weight * residual
        applied.append(value)
        squares = squares + jnp.sum(residual * residual)
        mixed = mixed + jnp.sum(residual * value)
    totals = jnp.stack([squares, mixed])
    for axis in ("mp", "tok", "heads"):
        totals = total_over(totals, axis)
    step_size = totals[0] / totals[1]
    residual = jnp.concatenate(residuals, 0)
    return (
        gram_new,
        cross_new,
        map_old + step_size * residual,
        residual - step_size * jnp.concatenate(applied, 0),
    )


UNITS = 16
LATER = 48
AHEAD = 2
MESH = pl.DeviceIdType.MESH


def gather_kernel(
    ctx, g_ref, m_hbm, w_hbm, skip_hbm, cross_hbm, map_hbm,
    panel, res_hbm, app_hbm, src_hbm, cols_hbm,
    maps, rf, acc, prod, buf, col, base, old, part, ry, rz, pair, cols, states, ip_send, ip_recv, delta, inner,
    own_sem, put_sem, in_sem, col_sem, out_sem, zs, zr, ys, yr, bs, br, cs, cr, xs, xr, mx, sy, sz, sc, sx, gz, gy, gc, ix,
):
    k, h, t = lax.axis_index("mp"), lax.axis_index("heads"), lax.axis_index("tok")
    z, y = h // 2, h % 2
    height, width = g_ref.shape[0] * g_ref.shape[1], g_ref.shape[2]
    unit = height // UNITS
    early = unit - LATER
    chunks = rf.shape[0] // 2
    per = UNITS // chunks
    step = height // chunks
    steps = ((1, 0), (-1, 1))
    new_weight = (1.0 - decay_keep) / ctx.shape[0]
    half_rows = pl.ds(pl.multiple_of(k * (step // 2), step // 2), step // 2)

    def block(zz, yy):
        return k * 8 + zz * 2 + yy

    def inside(zz):
        return (zz >= 0) & (zz <= 3)

    def piece(zz, yy, u, lo, n):
        return panel.at[block(zz, yy), pl.ds(pl.multiple_of(u * unit, unit) + lo, n)]

    def remote(ref, send, recv, dev):
        return pltpu.make_async_remote_copy(
            src_ref=ref, dst_ref=ref, send_sem=send, recv_sem=recv, device_id=dev, device_id_type=MESH
        )

    def at_z(dz):
        return (k, jnp.clip(z + dz, 0, 3) * 2 + y, t)

    at_y = (k, z * 2 + 1 - y, t)
    at_core = (1 - k, h, t)
    at_x = (k, h, 1 - t)

    def z_copy(s, dz, d, zz, u):
        return remote(piece(jnp.clip(zz, 0, 3), y, u, 0, unit), zs.at[d, s, u], zr.at[d, s, u], at_z(dz))

    def b_copy(s, dz, d, zz, u):
        return remote(
            piece(jnp.clip(zz, 0, 3), 1 - y, u, early, LATER), bs.at[d, s, u], br.at[d, s, u], at_z(dz)
        )

    def y_copy(zz, yy, u, n):
        zz = jnp.clip(zz, 0, 3)
        return remote(piece(zz, yy, u, 0, n), ys.at[zz, u], yr.at[zz, u], at_y)

    def core_copy(kk, u):
        ref = panel.at[pl.ds(kk * 8, 8), pl.ds(pl.multiple_of(u * unit, unit), unit)]
        return remote(ref, cs.at[u], cr.at[u], at_core)

    def x_copy(tt, c):
        return remote(rf.at[tt * chunks + c], xs.at[c], xr.at[c], at_x)

    def send_maps(tt):
        return remote(maps.at[pl.ds(tt * chunks, chunks)], mx.at[0], mx.at[1], at_x)

    def part_y(yy):
        return pltpu.make_async_remote_copy(
            src_ref=part.at[yy], dst_ref=ry, send_sem=sy.at[0], recv_sem=sy.at[1],
            device_id=at_y, device_id_type=MESH,
        )

    def line(zz):
        return (k, zz * 2 + y, t)

    def part_z(zz, to):
        return pltpu.make_async_remote_copy(
            src_ref=part.at[y, to], dst_ref=rz.at[zz], send_sem=sz.at[0, to], recv_sem=sz.at[1, zz],
            device_id=line(to), device_id_type=MESH,
        )

    def pair_core(kk):
        return remote(pair.at[kk], sc.at[0], sc.at[1], at_core)

    def pair_x():
        return pltpu.make_async_remote_copy(
            src_ref=pair, dst_ref=cols, send_sem=sx.at[0], recv_sem=sx.at[1],
            device_id=at_x, device_id_type=MESH,
        )

    def source_z(zz, to):
        return remote(states.at[y, zz, half_rows], gz.at[0, to], gz.at[1, zz], line(to))

    def source_y(yy):
        return remote(states.at[yy, :, half_rows], gy.at[0], gy.at[1], at_y)

    def source_core(kk):
        rows = pl.ds(pl.multiple_of(kk * (step // 2), step // 2), step // 2)
        return remote(states.at[:, :, rows], gc.at[0], gc.at[1], at_core)

    def inner_x(n):
        return pltpu.make_async_remote_copy(
            src_ref=ip_send.at[n], dst_ref=ip_recv.at[n], send_sem=ix.at[0, n], recv_sem=ix.at[1, n],
            device_id=at_x, device_id_type=MESH,
        )

    def feature(c):
        return states[c % 2, c // 2]

    def low_rank(c):
        return lax.dot_general(feature(c), delta[...], (((0,), (0,)), ((), ())), preferred_element_type=f32)

    own = pltpu.make_async_copy(g_ref, buf.at[pl.ds(0, chunks)], own_sem)
    own.start()
    load_maps = pltpu.make_async_copy(m_hbm, maps.at[pl.ds(t * chunks, chunks)], in_sem)
    load_maps.start()
    barrier = pltpu.get_barrier_semaphore()
    for dev in (at_y, at_core, at_x):
        pl.semaphore_signal(barrier, inc=1, device_id=dev, device_id_type=MESH)
    for dz in range(1, 4):
        pl.semaphore_signal(barrier, inc=1, device_id=line((z + dz) % 4), device_id_type=MESH)
    own.wait()

    def put(c):
        return pltpu.make_async_copy(
            buf.at[c], panel.at[block(z, y), pl.ds(c * step, step)], put_sem.at[c]
        )

    for c in range(8):
        put(c).start()
    load_maps.wait()
    pl.semaphore_wait(barrier, 6)
    for c in range(8):
        put(c).wait()
    send_maps(t).start()

    def valid(u):
        return (u >= 0) & (u < UNITS)

    def product_one(c):
        for part in range(per):
            core_copy(1 - k, per * c + part).wait_recv()
        rows = pl.ds(pl.multiple_of(c * step, step), step)
        load = pltpu.make_async_copy(panel.at[:, rows], buf, in_sem)
        load.start()
        load_base = pltpu.make_async_copy(cross_hbm.at[rows], base, own_sem)
        load_base.start()
        load_old = pltpu.make_async_copy(map_hbm.at[rows], old, col_sem.at[0, 0])
        load_old.start()
        load.wait()
        prod[...] = jnp.zeros_like(prod)

        @pl.loop(0, 8)
        def _(q):
            prod[...] += jnp.dot(buf[2 * q], maps[2 * q], preferred_element_type=f32) + jnp.dot(
                buf[2 * q + 1], maps[2 * q + 1], preferred_element_type=f32
            )

        load_base.wait()
        load_old.wait()
        base[...] = decay_keep * (base[...] - prod[...]) - ridge_weight * old[...] + new_weight * low_rank(c)
        rf[t * chunks + c] = base[...].astype(bf16)
        x_copy(t, c).start()
        save = pltpu.make_async_copy(base, res_hbm.at[rows], out_sem)
        save.start()
        prod[...] = jnp.zeros_like(prod)

        @pl.loop(0, c)
        def _(i):
            prod[...] += jnp.dot(buf[i], rf[i], preferred_element_type=f32) + jnp.dot(
                buf[chunks + i], rf[chunks + i], preferred_element_type=f32
            )

        acc[c] = prod[...]
        prod[...] = jnp.dot(feature(c), rf[t * chunks + c], preferred_element_type=f32)
        save.wait()

        @pl.when(c == 0)
        def _():
            inner[...] = prod[...]

        @pl.when(c > 0)
        def _():
            inner[...] += prod[...]

        @pl.when(c == chunks - 1)
        def _():
            ip_send[1] = inner[...].astype(bf16)
            inner_x(1).start()

    def column(c, i, slot, o):
        return pltpu.make_async_copy(
            panel.at[o * chunks + c, pl.ds(pl.multiple_of(i * step, step), step)],
            col.at[slot, o],
            col_sem.at[slot, o],
        )

    def product_two(c):
        for o in range(2):
            column(c, 0, 0, o).start()
        x_copy(1 - t, c).wait_recv()

        @pl.loop(0, c + 1)
        def _(i):
            slot = i % 2

            @pl.when(i < c)
            def _():
                for o in range(2):
                    column(c, i + 1, 1 - slot, o).start()

            for o in range(2):
                column(c, i, slot, o).wait()
            acc[i] += jnp.dot(col[slot, 0], rf[c], preferred_element_type=f32) + jnp.dot(
                col[slot, 1], rf[chunks + c], preferred_element_type=f32
            )

    @pl.loop(0, UNITS + 4 * AHEAD + per // 2 + 2)
    def _(tick):
        u0 = tick

        @pl.when(u0 < UNITS)
        def _():
            for dz, d in steps:
                @pl.when(inside(z + dz))
                def _():
                    z_copy(0, dz, d, z, u0).start()
            y_copy(z, y, u0, unit).start()

        for lag in range(1, 5):
            u = tick - lag * AHEAD

            @pl.when(valid(u))
            def _():
                if lag <= 3:
                    for dz, d in steps:
                        zz = z - lag * dz

                        @pl.when(inside(zz))
                        def _():
                            z_copy(lag - 1, dz, d, zz, u).wait_recv()
                            if lag < 3:
                                @pl.when(inside(z + dz))
                                def _():
                                    z_copy(lag, dz, d, zz, u).start()
                            y_copy(zz, y, u, early).start()
                if lag == 1:
                    y_copy(z, 1 - y, u, unit).wait_recv()
                    for dz, d in steps:
                        @pl.when(inside(z + dz))
                        def _():
                            b_copy(0, dz, d, z, u).start()
                else:
                    for dz, d in steps:
                        zz = z - (lag - 1) * dz

                        @pl.when(inside(zz))
                        def _():
                            y_copy(zz, 1 - y, u, early).wait_recv()
                            b_copy(lag - 2, dz, d, zz, u).wait_recv()
                            if lag < 4:
                                @pl.when(inside(z + dz))
                                def _():
                                    b_copy(lag - 1, dz, d, zz, u).start()
                if lag == 4:
                    core_copy(k, u).start()

        @pl.when(tick == 0)
        def _():
            def weights(i, slot, o):
                return pltpu.make_async_copy(
                    w_hbm.at[pl.ds(o * step, step), pl.ds(pl.multiple_of(i * step, step), step)],
                    col.at[slot, o],
                    col_sem.at[slot, o],
                )

            for o in range(2):
                weights(0, 0, o).start()

            @pl.loop(0, 8)
            def _(i):
                slot = i % 2

                @pl.when(i < 7)
                def _():
                    for o in range(2):
                        weights(i + 1, 1 - slot, o).start()

                for o in range(2):
                    weights(i, slot, o).wait()
                part[i % 2, i // 2] = (
                    jnp.dot(ctx[:, :step], col[slot, 0], preferred_element_type=f32)
                    + jnp.dot(ctx[:, step:], col[slot, 1], preferred_element_type=f32)
                ).astype(bf16)

            part_y(1 - y).start()

        @pl.when(tick == 4)
        def _():
            part_y(1 - y).wait_send()
            part_y(1 - y).wait_recv()

            @pl.loop(0, 4)
            def _(i):
                part[y, i] = (part[y, i].astype(f32) + ry[i].astype(f32)).astype(bf16)

            for dz in range(1, 4):
                part_z(z, (z + dz) % 4).start()

        @pl.when(tick == 6)
        def _():
            load = pltpu.make_async_copy(
                skip_hbm.at[k, :, pl.ds(pl.multiple_of(h * step, step), step)], delta, own_sem
            )
            load.start()
            total = part[y, z].astype(f32)
            for dz in range(1, 4):
                part_z((z + dz) % 4, z).wait_recv()
                total = total + rz[(z + dz) % 4].astype(f32)
            load.wait()
            pair[k] = (total + delta[...].astype(f32)).astype(bf16)
            pair_core(k).start()
            pair_core(1 - k).wait_recv()
            states[y, z, half_rows] = pair[0, half_rows]
            for dz in range(1, 4):
                source_z(z, (z + dz) % 4).start()

            @pl.when(k == t)
            def _():
                pair_x().start()
                cols[...] = pair[...]

        @pl.when(tick == 8)
        def _():
            for dz in range(1, 4):
                source_z((z + dz) % 4, z).wait_recv()
            source_y(y).start()

        @pl.when(tick == 9)
        def _():
            source_y(1 - y).wait_recv()
            source_core(k).start()
            source_core(1 - k).wait_recv()
            prod[...] = jnp.zeros_like(prod)

            @pl.loop(0, chunks)
            def _(c):
                prod[...] += jnp.dot(feature(c), maps[t * chunks + c], preferred_element_type=f32)

            ip_send[0] = prod[...].astype(bf16)
            inner_x(0).start()

        @pl.when(tick == 11)
        def _():
            @pl.when(k != t)
            def _():
                pair_x().wait_recv()

            inner_x(0).wait_recv()
            delta[...] = (cols[1].astype(f32) - prod[...] - ip_recv[0].astype(f32)).astype(bf16)
            send_maps(1 - t).wait_recv()

        w = tick - 4 * AHEAD - per - 1

        @pl.when((w >= 0) & (w % per == 0))
        def _():
            product_one(w // per)

        @pl.when((w >= 0) & (w % per == per // 2))
        def _():
            product_two(w // per)

    inner_x(1).wait_recv()
    delta[...] = (inner[...] + ip_recv[1].astype(f32)).astype(bf16)

    @pl.loop(0, chunks)
    def _(c):
        acc[c] = decay_keep * acc[c] + new_weight * low_rank(c)

    save = pltpu.make_async_copy(acc, app_hbm, out_sem)
    save.start()
    save_source = pltpu.make_async_copy(states, src_hbm, own_sem)
    save_source.start()
    save_cols = pltpu.make_async_copy(cols, cols_hbm, in_sem)
    save_cols.start()
    send_maps(t).wait_send()
    for dz in range(1, 4):
        part_z(z, (z + dz) % 4).wait_send()
        source_z(z, (z + dz) % 4).wait_send()
    pair_core(k).wait_send()
    source_y(y).wait_send()
    source_core(k).wait_send()
    for n in range(2):
        inner_x(n).wait_send()

    @pl.when(k == t)
    def _():
        pair_x().wait_send()

    @pl.loop(0, UNITS)
    def _(u):
        for s in range(3):
            for dz, d in steps:
                @pl.when(inside(z - s * dz) & inside(z + dz))
                def _():
                    z_copy(s, dz, d, z - s * dz, u).wait_send()
                    b_copy(s, dz, d, z - s * dz, u).wait_send()
        y_copy(z, y, u, unit).wait_send()
        for s in range(1, 4):
            for dz, d in steps:
                @pl.when(inside(z - s * dz))
                def _():
                    y_copy(z - s * dz, y, u, early).wait_send()
        core_copy(k, u).wait_send()

    @pl.loop(0, chunks)
    def _(c):
        x_copy(t, c).wait_send()

    save.wait()
    save_source.wait()
    save_cols.wait()


def gather_and_multiply(context, gram_half, map_half, out_weight, skip_states, cross_old, map_old):
    height, width = gram_half.shape
    chunks = 8
    step = height // chunks
    any_space = pl.BlockSpec(memory_space=pltpu.HBM)
    dma = pltpu.SemaphoreType.DMA
    tile = (step, width)
    _, residual, product, source, cols = pl.pallas_call(
        gather_kernel,
        out_shape=[
            jax.ShapeDtypeStruct((16, height, width), bf16),
            jax.ShapeDtypeStruct((height, width), f32),
            jax.ShapeDtypeStruct((chunks, *tile), f32),
            jax.ShapeDtypeStruct((2, 4, *tile), bf16),
            jax.ShapeDtypeStruct((2, *tile), bf16),
        ],
        in_specs=[pl.BlockSpec(memory_space=pltpu.VMEM)] + [any_space] * 6,
        out_specs=[any_space] * 5,
        scratch_shapes=[
            pltpu.VMEM((16, *tile), bf16),
            pltpu.VMEM((16, *tile), bf16),
            pltpu.VMEM((chunks, *tile), f32),
            pltpu.VMEM(tile, f32),
            pltpu.VMEM((16, *tile), bf16),
            pltpu.VMEM((2, 2, *tile), bf16),
            pltpu.VMEM(tile, f32),
            pltpu.VMEM(tile, f32),
            pltpu.VMEM((2, 4, *tile), bf16),
            pltpu.VMEM((4, *tile), bf16),
            pltpu.VMEM((4, *tile), bf16),
            pltpu.VMEM((2, *tile), bf16),
            pltpu.VMEM((2, *tile), bf16),
            pltpu.VMEM((2, 4, *tile), bf16),
            pltpu.VMEM((2, *tile), bf16),
            pltpu.VMEM((2, *tile), bf16),
            pltpu.VMEM(tile, bf16),
            pltpu.VMEM(tile, f32),
            dma, dma((chunks,)), dma, dma((2, 2)), dma,
            dma((2, 3, UNITS)), dma((2, 3, UNITS)),
            dma((4, UNITS)), dma((4, UNITS)),
            dma((2, 3, UNITS)), dma((2, 3, UNITS)),
            dma((UNITS,)), dma((UNITS,)),
            dma((chunks,)), dma((chunks,)),
            dma((2,)), dma((2,)), dma((2, 4)), dma((2,)), dma((2,)), dma((2, 4)), dma((2,)), dma((2,)), dma((2, 2)),
        ],
        compiler_params=pltpu.CompilerParams(
            collective_id=0, has_side_effects=True, vmem_limit_bytes=60 * 1024 * 1024
        ),
    )(
        context, gram_half.reshape(chunks, *tile), map_half.reshape(chunks, *tile),
        out_weight, skip_states, cross_old, map_old,
    )
    return residual, product.reshape(height, width), source, cols


def with_kernel(context, out_weight, skip_states, gram_old, cross_old, map_old):
    tokens = context.shape[1]
    height, width = gram_old.shape
    new_weight = (1.0 - decay_keep) / tokens
    residual, product, source, cols = gather_and_multiply(
        context[0], gram_old.astype(bf16), map_old.astype(bf16), out_weight[0], skip_states, cross_old, map_old
    )
    source = jnp.concatenate([source[i % 2, i // 2] for i in range(8)], 1)
    gram_new = decay_keep * gram_old + new_weight * token_inner(source, cols[0])
    cross_new = decay_keep * cross_old + new_weight * token_inner(source, cols[1])
    applied = product + ridge_weight * residual
    totals = jnp.stack([jnp.sum(residual * residual), jnp.sum(residual * applied)])
    for axis in ("mp", "tok", "heads"):
        totals = total_over(totals, axis)
    step_size = totals[0] / totals[1]
    return gram_new, cross_new, map_old + step_size * residual, residual - step_size * applied


def solution(mesh):
    block = P("tok", ("mp", "heads"))
    placed = (P("mp", None, "heads"), P("mp", "heads", "tok"), P(None, None, "tok"), block, block, block)
    lines = dict(mesh.shape) == {"mp": 2, "heads": 8, "tok": 2}
    return jax.shard_map(
        with_kernel if lines else per_device,
        mesh=mesh, in_specs=placed, out_specs=(block,) * 4, check_vma=False,
    )
```

```python
import jax
import jax.numpy as jnp
from jax import lax
from jax.experimental import pallas as pl
from jax.experimental.pallas import tpu as pltpu
from jax.sharding import PartitionSpec as P

decay_keep = 0.75
ridge_weight = 0.1
f32, bf16 = jnp.float32, jnp.bfloat16
CHUNKS = 4


def dot(a, b):
    return jnp.dot(a, b, preferred_element_type=f32)


def token_inner(left, right):
    return lax.dot_general(left, right, (((0,), (0,)), ((), ())), preferred_element_type=f32)


def shifted(block, axis, shift):
    n = lax.axis_size(axis)
    return lax.ppermute(block, axis, [(i, (i + shift) % n) for i in range(n)])


def total_over(value, axis):
    n = lax.axis_size(axis)
    if n & (n - 1):
        return lax.psum(value, axis)
    bit = 1
    while bit < n:
        value = value + lax.ppermute(value, axis, [(i, i ^ bit) for i in range(n)])
        bit *= 2
    return value


def sum_tok(value):
    n = lax.axis_size("tok")
    half = value.astype(bf16)
    for shift in range(1, n):
        value = value + shifted(half, "tok", shift).astype(f32)
    return value.astype(bf16)


def scatter_sum(part, axis):
    n = lax.axis_size(axis)
    me = lax.axis_index(axis)
    share = part.shape[1] // n
    blocks = [part[:, i * share:(i + 1) * share] for i in range(n)]
    bit = 1
    while bit < n:
        mine = (me // bit) % 2 == 1
        keep = [jnp.where(mine, high, low) for low, high in zip(blocks[0::2], blocks[1::2])]
        send = [jnp.where(mine, low, high) for low, high in zip(blocks[0::2], blocks[1::2])]
        send = jnp.concatenate([block.astype(bf16) for block in send], 1)
        got = lax.ppermute(send, axis, [(i, i ^ bit) for i in range(n)]).astype(f32)
        blocks = [block.astype(f32) + got[:, i * share:(i + 1) * share] for i, block in enumerate(keep)]
        bit *= 2
    return blocks[0]


def gather_columns(block, axis):
    n = lax.axis_size(axis)
    me = lax.axis_index(axis)
    bit = n // 2
    blocks = [block]
    while bit:
        mine = (me // bit) % 2 == 1
        own = jnp.concatenate(blocks, 1)
        got = lax.ppermute(own, axis, [(i, i ^ bit) for i in range(n)])
        share = block.shape[1]
        got = [got[:, i * share:(i + 1) * share] for i in range(len(blocks))]
        low = [jnp.where(mine, g, o) for g, o in zip(got, blocks)]
        high = [jnp.where(mine, o, g) for g, o in zip(got, blocks)]
        blocks = [x for pair in zip(low, high) for x in pair]
        bit //= 2
    return jnp.concatenate(blocks, 1)


def make_states(context, out_weight, skip_states, width):
    n_tok, n_heads, n_mp = (lax.axis_size(a) for a in ("tok", "heads", "mp"))
    t, h, k = (lax.axis_index(a) for a in ("tok", "heads", "mp"))
    tokens, features = skip_states.shape[1:]
    share = features // n_heads
    part = dot(context[0], out_weight[0]).astype(bf16)
    mine = scatter_sum(part, "heads")
    skip = lax.dynamic_slice(skip_states, (k, 0, h * share), (1, tokens, share))[0]
    mine = (mine + skip.astype(f32)).astype(bf16)
    other = lax.ppermute(mine, "mp", [(0, 1), (1, 0)])
    pair = jnp.stack([jnp.where(k == 0, mine, other), jnp.where(k == 0, other, mine)])
    if share == width and n_tok == n_mp == 2:
        away = lax.ppermute(pair, ("mp", "tok"), [(0, 1), (3, 2)])
        columns = jnp.where(k == t, pair, away)
        half = lax.dynamic_slice_in_dim(pair[0], k * (tokens // 2), tokens // 2, 0)
        rows = gather_columns(half, "heads")
        rows_other = lax.ppermute(rows, "mp", [(0, 1), (1, 0)])
        first = jnp.where(k == 0, rows, rows_other)
        second = jnp.where(k == 0, rows_other, rows)
        source = jnp.concatenate([first, second], 0)
        return source, columns[0], columns[1]
    both = lax.all_gather(pair, "heads", axis=2, tiled=True)
    whole = lax.all_gather(both, "tok", axis=2, tiled=True)
    columns = lax.dynamic_slice_in_dim(whole, (k * n_heads + h) * width, width, 2)
    return both[0], columns[0], columns[1]


def per_device(context, out_weight, skip_states, gram_old, cross_old, map_old):
    n_tok = lax.axis_size("tok")
    t = lax.axis_index("tok")
    tokens = context.shape[1]
    height, width = gram_old.shape
    new_weight = (1.0 - decay_keep) / tokens
    step = height // CHUNKS
    cuts = [slice(c * step, (c + 1) * step) for c in range(CHUNKS)]

    map_half = map_old.astype(bf16)
    gram_old_half = gram_old.astype(bf16)
    gram_old_half, context = lax.optimization_barrier((gram_old_half, context))
    panel = lax.all_gather(gram_old_half, ("mp", "heads"), axis=1, tiled=True)
    maps = [map_half] + [shifted(map_half, "tok", s) for s in range(1, n_tok)]
    source, source_cols, target_cols = make_states(context, out_weight, skip_states, width)

    gram_new = decay_keep * gram_old + new_weight * token_inner(source, source_cols)
    cross_new = decay_keep * cross_old + new_weight * token_inner(source, target_cols)

    def panel_part(cut, s):
        owner = lax.rem(t - s + n_tok, n_tok)
        return lax.dynamic_slice(panel, (cut.start, owner * height), (step, height))

    inner_map = sum_tok(dot(source, map_half))
    residuals, halves = [], []
    for cut in cuts:
        product = sum(dot(panel_part(cut, s), maps[s]) for s in range(n_tok))
        low_rank = token_inner(source[:, cut], inner_map)
        residual = (
            cross_new[cut] - decay_keep * product - new_weight * low_rank - ridge_weight * map_old[cut]
        )
        residuals.append(residual)
        halves.append(residual.astype(bf16))
    away = [[shifted(half, "tok", s) for half in halves] for s in range(1, n_tok)]
    inner_residual = sum_tok(sum(dot(source[:, cut], half) for cut, half in zip(cuts, halves)))
    blocks = [jnp.concatenate(halves, 0)] + [jnp.concatenate(a, 0) for a in away]
    applied, squares, mixed = [], 0.0, 0.0
    for cut, residual in zip(cuts, residuals):
        product = sum(dot(panel_part(cut, s), blocks[s]) for s in range(n_tok))
        low_rank = token_inner(source[:, cut], inner_residual)
        value = decay_keep * product + new_weight * low_rank + ridge_weight * residual
        applied.append(value)
        squares = squares + jnp.sum(residual * residual)
        mixed = mixed + jnp.sum(residual * value)
    totals = jnp.stack([squares, mixed])
    for axis in ("mp", "tok", "heads"):
        totals = total_over(totals, axis)
    step_size = totals[0] / totals[1]
    residual = jnp.concatenate(residuals, 0)
    return (
        gram_new,
        cross_new,
        map_old + step_size * residual,
        residual - step_size * jnp.concatenate(applied, 0),
    )


UNITS = 16
LATER = 48
AHEAD = 1
EARLY = 1
PHASES = (3, 5, 6, 7, 9)
MESH = pl.DeviceIdType.MESH


def gather_kernel(
    ctx, g_ref, m_hbm, w_hbm, skip_hbm, cross_hbm, map_hbm,
    panel, res_hbm, app_hbm, src_hbm, cols_hbm,
    maps, rf, acc, prod, buf, col, base, old, part, ry, rz, pair, cols, states, ip_send, ip_recv, delta, inner,
    own_sem, put_sem, in_sem, col_sem, out_sem, zs, zr, ys, yr, bs, br, cs, cr, xs, xr, mx, sy, sz, sc, sx, gz, gy, gc, ix,
):
    k, h, t = lax.axis_index("mp"), lax.axis_index("heads"), lax.axis_index("tok")
    z, y = h // 2, h % 2
    height, width = g_ref.shape[0] * g_ref.shape[1], g_ref.shape[2]
    unit = height // UNITS
    early = unit - LATER
    chunks = rf.shape[0] // 2
    per = UNITS // chunks
    step = height // chunks
    steps = ((1, 0), (-1, 1))
    new_weight = (1.0 - decay_keep) / ctx.shape[0]
    half_rows = pl.ds(pl.multiple_of(k * (step // 2), step // 2), step // 2)

    def block(zz, yy):
        return k * 8 + zz * 2 + yy

    def inside(zz):
        return (zz >= 0) & (zz <= 3)

    def piece(zz, yy, u, lo, n):
        return panel.at[block(zz, yy), pl.ds(pl.multiple_of(u * unit, unit) + lo, n)]

    def remote(ref, send, recv, dev):
        return pltpu.make_async_remote_copy(
            src_ref=ref, dst_ref=ref, send_sem=send, recv_sem=recv, device_id=dev, device_id_type=MESH
        )

    def at_z(dz):
        return (k, jnp.clip(z + dz, 0, 3) * 2 + y, t)

    at_y = (k, z * 2 + 1 - y, t)
    at_core = (1 - k, h, t)
    at_x = (k, h, 1 - t)

    def own_copy(u, send, recv, dev):
        return pltpu.make_async_remote_copy(
            src_ref=g_ref.at[u // per, pl.ds(pl.multiple_of((u % per) * unit, unit), unit)],
            dst_ref=piece(z, y, u, 0, unit),
            send_sem=send, recv_sem=recv, device_id=dev, device_id_type=MESH,
        )

    def send_own(u):
        for dz, d in steps:
            @pl.when(inside(z + dz))
            def _():
                own_copy(u, zs.at[d, 0, u], zr.at[d, 0, u], at_z(dz)).start()
        own_copy(u, ys.at[z, u], yr.at[z, u], at_y).start()

    def z_copy(s, dz, d, zz, u):
        return remote(piece(jnp.clip(zz, 0, 3), y, u, 0, unit), zs.at[d, s, u], zr.at[d, s, u], at_z(dz))

    def b_copy(s, dz, d, zz, u):
        return remote(
            piece(jnp.clip(zz, 0, 3), 1 - y, u, early, LATER), bs.at[d, s, u], br.at[d, s, u], at_z(dz)
        )

    def y_copy(zz, yy, u, n):
        zz = jnp.clip(zz, 0, 3)
        return remote(piece(zz, yy, u, 0, n), ys.at[zz, u], yr.at[zz, u], at_y)

    def core_copy(kk, u):
        ref = panel.at[pl.ds(kk * 8, 8), pl.ds(pl.multiple_of(u * unit, unit), unit)]
        return remote(ref, cs.at[u], cr.at[u], at_core)

    def x_copy(tt, c):
        return remote(rf.at[tt * chunks + c], xs.at[c], xr.at[c], at_x)

    def send_maps(tt):
        return remote(maps.at[pl.ds(tt * chunks, chunks)], mx.at[0], mx.at[1], at_x)

    def part_y(yy):
        return pltpu.make_async_remote_copy(
            src_ref=part.at[yy], dst_ref=ry, send_sem=sy.at[0], recv_sem=sy.at[1],
            device_id=at_y, device_id_type=MESH,
        )

    def line(zz):
        return (k, zz * 2 + y, t)

    def part_z(zz, to):
        return pltpu.make_async_remote_copy(
            src_ref=part.at[y, to], dst_ref=rz.at[zz], send_sem=sz.at[0, to], recv_sem=sz.at[1, zz],
            device_id=line(to), device_id_type=MESH,
        )

    def pair_core(kk):
        return remote(pair.at[kk], sc.at[0], sc.at[1], at_core)

    def pair_x():
        return pltpu.make_async_remote_copy(
            src_ref=pair, dst_ref=cols, send_sem=sx.at[0], recv_sem=sx.at[1],
            device_id=at_x, device_id_type=MESH,
        )

    def source_z(zz, to):
        return remote(states.at[y, zz, half_rows], gz.at[0, to], gz.at[1, zz], line(to))

    def source_y(yy):
        return remote(states.at[yy, :, half_rows], gy.at[0], gy.at[1], at_y)

    def source_core(kk):
        rows = pl.ds(pl.multiple_of(kk * (step // 2), step // 2), step // 2)
        return remote(states.at[:, :, rows], gc.at[0], gc.at[1], at_core)

    def inner_x(n):
        return pltpu.make_async_remote_copy(
            src_ref=ip_send.at[n], dst_ref=ip_recv.at[n], send_sem=ix.at[0, n], recv_sem=ix.at[1, n],
            device_id=at_x, device_id_type=MESH,
        )

    def feature(c):
        return states[c % 2, c // 2]

    def low_rank(c):
        return lax.dot_general(feature(c), delta[...], (((0,), (0,)), ((), ())), preferred_element_type=f32)

    own = pltpu.make_async_copy(g_ref, buf.at[pl.ds(0, chunks)], own_sem)
    own.start()
    load_maps = pltpu.make_async_copy(m_hbm, maps.at[pl.ds(t * chunks, chunks)], in_sem)
    load_maps.start()
    barrier = pltpu.get_barrier_semaphore()
    for dev in (at_y, at_core, at_x):
        pl.semaphore_signal(barrier, inc=1, device_id=dev, device_id_type=MESH)
    for dz in range(1, 4):
        pl.semaphore_signal(barrier, inc=1, device_id=line((z + dz) % 4), device_id_type=MESH)

    def put(c):
        return pltpu.make_async_copy(
            buf.at[c], panel.at[block(z, y), pl.ds(c * step, step)], put_sem.at[c]
        )

    pl.semaphore_wait(barrier, 6)
    for u in range(EARLY):
        send_own(u)

    def valid(u):
        return (u >= 0) & (u < UNITS)

    def product_one(c):
        for part in range(per):
            core_copy(1 - k, per * c + part).wait_recv()
        rows = pl.ds(pl.multiple_of(c * step, step), step)
        load = pltpu.make_async_copy(panel.at[:, rows], buf, in_sem)
        load.start()
        load_base = pltpu.make_async_copy(cross_hbm.at[rows], base, own_sem)
        load_base.start()
        load_old = pltpu.make_async_copy(map_hbm.at[rows], old, col_sem.at[0, 0])
        load_old.start()
        load.wait()
        prod[...] = jnp.zeros_like(prod)

        @pl.loop(0, 4)
        def _(q):
            prod[...] += sum(
                jnp.dot(buf[4 * q + i], maps[4 * q + i], preferred_element_type=f32) for i in range(4)
            )

        load_base.wait()
        load_old.wait()
        base[...] = decay_keep * (base[...] - prod[...]) - ridge_weight * old[...] + new_weight * low_rank(c)
        rf[t * chunks + c] = base[...].astype(bf16)
        x_copy(t, c).start()
        save = pltpu.make_async_copy(base, res_hbm.at[rows], out_sem)
        save.start()
        prod[...] = jnp.zeros_like(prod)

        @pl.loop(0, c)
        def _(i):
            prod[...] += jnp.dot(buf[i], rf[i], preferred_element_type=f32) + jnp.dot(
                buf[chunks + i], rf[chunks + i], preferred_element_type=f32
            )

        acc[c] = prod[...]
        prod[...] = jnp.dot(feature(c), rf[t * chunks + c], preferred_element_type=f32)
        save.wait()

        @pl.when(c == 0)
        def _():
            inner[...] = prod[...]

        @pl.when(c > 0)
        def _():
            inner[...] += prod[...]

        @pl.when(c == chunks - 1)
        def _():
            ip_send[1] = inner[...].astype(bf16)
            inner_x(1).start()

    def column(c, i, slot, o):
        return pltpu.make_async_copy(
            panel.at[o * chunks + c, pl.ds(pl.multiple_of(i * step, step), step)],
            col.at[slot, o],
            col_sem.at[slot, o],
        )

    def product_two(c):
        for o in range(2):
            column(c, 0, 0, o).start()
        x_copy(1 - t, c).wait_recv()

        @pl.loop(0, c + 1)
        def _(i):
            slot = i % 2

            @pl.when(i < c)
            def _():
                for o in range(2):
                    column(c, i + 1, 1 - slot, o).start()

            for o in range(2):
                column(c, i, slot, o).wait()
            acc[i] += jnp.dot(col[slot, 0], rf[c], preferred_element_type=f32) + jnp.dot(
                col[slot, 1], rf[chunks + c], preferred_element_type=f32
            )

    @pl.loop(0, UNITS + 4 * AHEAD + per)
    def _(tick):
        @pl.when(tick + EARLY < UNITS)
        def _():
            send_own(tick + EARLY)

        for lag in range(1, 5):
            u = tick - lag * AHEAD

            @pl.when(valid(u))
            def _():
                if lag <= 3:
                    for dz, d in steps:
                        zz = z - lag * dz

                        @pl.when(inside(zz))
                        def _():
                            z_copy(lag - 1, dz, d, zz, u).wait_recv()
                            if lag < 3:
                                @pl.when(inside(z + dz))
                                def _():
                                    z_copy(lag, dz, d, zz, u).start()
                            y_copy(zz, y, u, early).start()
                if lag == 1:
                    y_copy(z, 1 - y, u, unit).wait_recv()
                    for dz, d in steps:
                        @pl.when(inside(z + dz))
                        def _():
                            b_copy(0, dz, d, z, u).start()
                else:
                    for dz, d in steps:
                        zz = z - (lag - 1) * dz

                        @pl.when(inside(zz))
                        def _():
                            y_copy(zz, 1 - y, u, early).wait_recv()
                            b_copy(lag - 2, dz, d, zz, u).wait_recv()
                            if lag < 4:
                                @pl.when(inside(z + dz))
                                def _():
                                    b_copy(lag - 1, dz, d, zz, u).start()
                if lag == 4:
                    core_copy(k, u).start()

        @pl.when(tick == 0)
        def _():
            def weights(i, slot, o):
                return pltpu.make_async_copy(
                    w_hbm.at[pl.ds(o * step, step), pl.ds(pl.multiple_of(i * step, step), step)],
                    col.at[slot, o],
                    col_sem.at[slot, o],
                )

            for o in range(2):
                weights(0, 0, o).start()
            own.wait()
            for c in range(8):
                put(c).start()
            load_maps.wait()
            send_maps(t).start()

            @pl.loop(0, 8)
            def _(i):
                slot = i % 2

                @pl.when(i < 7)
                def _():
                    for o in range(2):
                        weights(i + 1, 1 - slot, o).start()

                for o in range(2):
                    weights(i, slot, o).wait()
                part[i % 2, i // 2] = (
                    jnp.dot(ctx[:, :step], col[slot, 0], preferred_element_type=f32)
                    + jnp.dot(ctx[:, step:], col[slot, 1], preferred_element_type=f32)
                ).astype(bf16)

            part_y(1 - y).start()
            for c in range(8):
                put(c).wait()

        @pl.when(tick == PHASES[0])
        def _():
            part_y(1 - y).wait_send()
            part_y(1 - y).wait_recv()

            @pl.loop(0, 4)
            def _(i):
                part[y, i] = (part[y, i].astype(f32) + ry[i].astype(f32)).astype(bf16)

            for dz in range(1, 4):
                part_z(z, (z + dz) % 4).start()

        @pl.when(tick == PHASES[1])
        def _():
            load = pltpu.make_async_copy(
                skip_hbm.at[k, :, pl.ds(pl.multiple_of(h * step, step), step)], delta, own_sem
            )
            load.start()
            total = part[y, z].astype(f32)
            for dz in range(1, 4):
                part_z((z + dz) % 4, z).wait_recv()
                total = total + rz[(z + dz) % 4].astype(f32)
            load.wait()
            pair[k] = (total + delta[...].astype(f32)).astype(bf16)
            pair_core(k).start()
            pair_core(1 - k).wait_recv()
            states[y, z, half_rows] = pair[0, half_rows]
            for dz in range(1, 4):
                source_z(z, (z + dz) % 4).start()

            @pl.when(k == t)
            def _():
                pair_x().start()
                cols[...] = pair[...]

        @pl.when(tick == PHASES[2])
        def _():
            for dz in range(1, 4):
                source_z((z + dz) % 4, z).wait_recv()
            source_y(y).start()

        @pl.when(tick == PHASES[3])
        def _():
            source_y(1 - y).wait_recv()
            source_core(k).start()
            source_core(1 - k).wait_recv()
            prod[...] = jnp.zeros_like(prod)

            @pl.loop(0, chunks)
            def _(c):
                prod[...] += jnp.dot(feature(c), maps[t * chunks + c], preferred_element_type=f32)

            ip_send[0] = prod[...].astype(bf16)
            inner_x(0).start()

        @pl.when(tick == PHASES[4])
        def _():
            @pl.when(k != t)
            def _():
                pair_x().wait_recv()

            inner_x(0).wait_recv()
            delta[...] = (cols[1].astype(f32) - prod[...] - ip_recv[0].astype(f32)).astype(bf16)
            send_maps(1 - t).wait_recv()

        first = PHASES[-1]
        behind = 2 * first - 6

        def chunk_of(at):
            busy = (at >= first) & ((at <= behind) | (at % 2 == 0)) & (at < 2 * chunks + 6)
            return busy, jnp.where(at <= behind, at - first, (at - 6) // 2)

        busy_two, chunk_two = chunk_of(tick - 1)

        @pl.when(busy_two)
        def _():
            product_two(chunk_two)

        busy_one, chunk_one = chunk_of(tick)

        @pl.when(busy_one)
        def _():
            product_one(chunk_one)

    inner_x(1).wait_recv()
    delta[...] = (inner[...] + ip_recv[1].astype(f32)).astype(bf16)

    @pl.loop(0, chunks)
    def _(c):
        acc[c] = decay_keep * acc[c] + new_weight * low_rank(c)

    save = pltpu.make_async_copy(acc, app_hbm, out_sem)
    save.start()
    save_source = pltpu.make_async_copy(states, src_hbm, own_sem)
    save_source.start()
    save_cols = pltpu.make_async_copy(cols, cols_hbm, in_sem)
    save_cols.start()
    send_maps(t).wait_send()
    for dz in range(1, 4):
        part_z(z, (z + dz) % 4).wait_send()
        source_z(z, (z + dz) % 4).wait_send()
    pair_core(k).wait_send()
    source_y(y).wait_send()
    source_core(k).wait_send()
    for n in range(2):
        inner_x(n).wait_send()

    @pl.when(k == t)
    def _():
        pair_x().wait_send()

    @pl.loop(0, UNITS)
    def _(u):
        for s in range(3):
            for dz, d in steps:
                @pl.when(inside(z - s * dz) & inside(z + dz))
                def _():
                    z_copy(s, dz, d, z - s * dz, u).wait_send()
                    b_copy(s, dz, d, z - s * dz, u).wait_send()
        y_copy(z, y, u, unit).wait_send()
        for s in range(1, 4):
            for dz, d in steps:
                @pl.when(inside(z - s * dz))
                def _():
                    y_copy(z - s * dz, y, u, early).wait_send()
        core_copy(k, u).wait_send()

    @pl.loop(0, chunks)
    def _(c):
        x_copy(t, c).wait_send()

    save.wait()
    save_source.wait()
    save_cols.wait()


def gather_and_multiply(context, gram_half, map_half, out_weight, skip_states, cross_old, map_old):
    height, width = gram_half.shape
    chunks = 8
    step = height // chunks
    any_space = pl.BlockSpec(memory_space=pltpu.HBM)
    dma = pltpu.SemaphoreType.DMA
    tile = (step, width)
    _, residual, product, source, cols = pl.pallas_call(
        gather_kernel,
        out_shape=[
            jax.ShapeDtypeStruct((16, height, width), bf16),
            jax.ShapeDtypeStruct((height, width), f32),
            jax.ShapeDtypeStruct((chunks, *tile), f32),
            jax.ShapeDtypeStruct((2, 4, *tile), bf16),
            jax.ShapeDtypeStruct((2, *tile), bf16),
        ],
        in_specs=[pl.BlockSpec(memory_space=pltpu.VMEM)] + [any_space] * 6,
        out_specs=[any_space] * 5,
        scratch_shapes=[
            pltpu.VMEM((16, *tile), bf16),
            pltpu.VMEM((16, *tile), bf16),
            pltpu.VMEM((chunks, *tile), f32),
            pltpu.VMEM(tile, f32),
            pltpu.VMEM((16, *tile), bf16),
            pltpu.VMEM((2, 2, *tile), bf16),
            pltpu.VMEM(tile, f32),
            pltpu.VMEM(tile, f32),
            pltpu.VMEM((2, 4, *tile), bf16),
            pltpu.VMEM((4, *tile), bf16),
            pltpu.VMEM((4, *tile), bf16),
            pltpu.VMEM((2, *tile), bf16),
            pltpu.VMEM((2, *tile), bf16),
            pltpu.VMEM((2, 4, *tile), bf16),
            pltpu.VMEM((2, *tile), bf16),
            pltpu.VMEM((2, *tile), bf16),
            pltpu.VMEM(tile, bf16),
            pltpu.VMEM(tile, f32),
            dma, dma((chunks,)), dma, dma((2, 2)), dma,
            dma((2, 3, UNITS)), dma((2, 3, UNITS)),
            dma((4, UNITS)), dma((4, UNITS)),
            dma((2, 3, UNITS)), dma((2, 3, UNITS)),
            dma((UNITS,)), dma((UNITS,)),
            dma((chunks,)), dma((chunks,)),
            dma((2,)), dma((2,)), dma((2, 4)), dma((2,)), dma((2,)), dma((2, 4)), dma((2,)), dma((2,)), dma((2, 2)),
        ],
        compiler_params=pltpu.CompilerParams(
            collective_id=0, has_side_effects=True, vmem_limit_bytes=60 * 1024 * 1024
        ),
    )(
        context, gram_half.reshape(chunks, *tile), map_half.reshape(chunks, *tile),
        out_weight, skip_states, cross_old, map_old,
    )
    return residual, product.reshape(height, width), source, cols


def with_kernel(context, out_weight, skip_states, gram_old, cross_old, map_old):
    tokens = context.shape[1]
    height, width = gram_old.shape
    new_weight = (1.0 - decay_keep) / tokens
    residual, product, source, cols = gather_and_multiply(
        context[0], gram_old.astype(bf16), map_old.astype(bf16), out_weight[0], skip_states, cross_old, map_old
    )
    source = jnp.concatenate([source[i % 2, i // 2] for i in range(8)], 1)
    applied = product + ridge_weight * residual
    totals = jnp.stack([jnp.sum(residual * residual), jnp.sum(residual * applied)])
    totals = total_over(totals, "mp")
    totals, source_cols = lax.optimization_barrier((totals, cols[0]))
    gram_new = decay_keep * gram_old + new_weight * token_inner(source, source_cols)
    totals = total_over(totals, "tok")
    totals, target_cols = lax.optimization_barrier((totals, cols[1]))
    cross_new = decay_keep * cross_old + new_weight * token_inner(source, target_cols)
    totals = total_over(totals, "heads")
    step_size = totals[0] / totals[1]
    return gram_new, cross_new, map_old + step_size * residual, residual - step_size * applied


def solution(mesh):
    block = P("tok", ("mp", "heads"))
    placed = (P("mp", None, "heads"), P("mp", "heads", "tok"), P(None, None, "tok"), block, block, block)
    lines = dict(mesh.shape) == {"mp": 2, "heads": 8, "tok": 2}
    return jax.shard_map(
        with_kernel if lines else per_device,
        mesh=mesh, in_specs=placed, out_specs=(block,) * 4, check_vma=False,
    )
```
